256 devices in a mesh: window: 32 (over z, x_lo, core), token: 8 (over x_hi, y).
Axes of the slice: x: 4 (x_hi: 2, x_lo: 2; x = x_hi * 2 + x_lo), y: 4, z: 8, core: 2. Of those that a mesh axis runs over, the one named last changes fastest.
Arguments:
- latents: bfloat16 [32, 9, 128, 5120], P('window', None, 'token'), may hold values from -36 to 36
- queries: bfloat16 [32, 9, 128, 5120], P('window', None, 'token'), may hold values from -128 to 128
- attn_keys: bfloat16 [32, 9, 128, 5120], P('window', None, 'token'), may hold values from -4.5 to 4.5
- cached: bfloat16 [4, 32, 9, 128, 5120], P(None, 'window', None, 'token'), may hold values from -3 to 3
- plan: int32 [4], replicated, may hold values from 0 to 1
- refresh: int32 [32], replicated, may hold values from 0 to 3
- value_gain: float32 [5120], replicated, may hold values from 0.1 to 1.9
- attn_gate: float32 [5120], replicated, may hold values from 0.5 to 3
- intersections: int32 [32], replicated, may hold values from 1 to 4, as said below
Outputs:
- looped: bfloat16 [32, 9, 128, 5120], P('window', None, 'token')
The draws below stay inside these ranges and needn't reach their ends.
Inputs may be any that keep to these rules, and one draw needn't show every extreme that they name: `intersections`: some window has exactly 4.
All inputs are finite; a program needn't handle non-finite values.
Results may differ from the reference program's by a relative error of at most 0.0065.
Values may be sent and summed in bfloat16 or wider, within the bound.
No kernel may reach another device: no remote copies, remote signals or barrier semaphores. Data moves between devices by JAX's collectives and lax.ppermute only.
A program may use at most 128 MiB of HBM per device.

```python
import math
import jax
import jax.numpy as jnp
from jax import lax

HEADS = 40
HEAD_DIM = 128
D = 5120
FRAMES = 9
MAXOV = 4
BLOCKS = 4
SPATIAL = 128
WINDOWS = 32


def key_base(key):
    shape = (WINDOWS, FRAMES, SPATIAL, D)
    return jnp.clip(jax.random.normal(key, shape, jnp.float32), -4.5, 4.5)


def draw_attn_keys(key, part):
    base = key_base(key)
    return base.astype(jnp.bfloat16)


def draw_queries(key, part):
    key = jax.random.fold_in(key, 11)
    shape = (WINDOWS, FRAMES, SPATIAL, D)
    noise = jnp.clip(jax.random.normal(key, shape, jnp.float32), -4.5, 4.5) * 2.0
    return noise.astype(jnp.bfloat16)


def draw_latents(key, part):
    key = jax.random.fold_in(key, 3)
    key_noise, key_rows, key_cols = jax.random.split(key, 3)
    shape = (WINDOWS, FRAMES, SPATIAL, D)
    rows = jnp.exp(jax.random.uniform(key_rows, (WINDOWS, FRAMES, SPATIAL, 1), jnp.float32, math.log(0.3), math.log(3.0)))
    cols = jnp.exp(jax.random.uniform(key_cols, (D,), jnp.float32, math.log(0.3), math.log(3.0)))
    noise = jnp.clip(jax.random.normal(key_noise, shape, jnp.float32), -4.0, 4.0)
    return jnp.clip(noise * rows * cols, -36.0, 36.0).astype(jnp.bfloat16)


def draw_intersections(key, part):
    key = jax.random.fold_in(key, 5)
    key_counts, key_spot = jax.random.split(key)
    counts = jax.random.randint(key_counts, (WINDOWS,), 1, MAXOV + 1)
    spot = jax.random.randint(key_spot, (), 0, WINDOWS)
    return jnp.where(jnp.arange(WINDOWS) == spot, MAXOV, counts).astype(jnp.int32)


def draw_plan(key, part):
    key = jax.random.fold_in(key, 23)
    key_raw, key_order = jax.random.split(key)
    raw = jax.random.randint(key_raw, (BLOCKS,), 0, 3)
    sched = jnp.where(raw > 0, 1, 0)
    order = jax.random.permutation(key_order, BLOCKS)
    sched = sched.at[order[0]].set(1)
    sched = sched.at[order[1]].set(0)
    return sched.astype(jnp.int32)


def draw_refresh(key, part):
    key = jax.random.fold_in(key, 21)
    key_raw, key_order = jax.random.split(key)
    raw = jax.random.randint(key_raw, (WINDOWS,), 0, BLOCKS)
    order = jax.random.permutation(key_order, WINDOWS)
    raw = raw.at[order[0]].set(0)
    raw = raw.at[order[1]].set(BLOCKS - 1)
    return raw.astype(jnp.int32)


def levels(stream_key, dims, cuts, least, high):
    gain, own = 1.0, jax.random.fold_in(stream_key, 6)
    for position, parts in cuts:
        draws = jnp.exp(jax.random.uniform(jax.random.fold_in(own, position), (parts,), jnp.float32, least / len(cuts), high / len(cuts)))
        gain = gain * jnp.repeat(draws, dims[position] // parts).reshape([-1 if axis == position else 1 for axis in range(len(dims))])
    return gain


def gaussian(rng, shape, spread, bound, pieces=(), kind=jnp.bfloat16):
    loudness = levels(rng, shape, pieces, -0.22, 0.18) if pieces else 1.0
    drawn = jax.random.normal(rng, shape, jnp.float32) * spread * loudness
    return jnp.minimum(jnp.maximum(drawn, -bound), bound).astype(kind)


def setup_inputs(seed: int = 0) -> dict:
    streams_of = jax.random.split(jax.random.key(seed), 10)
    latents = draw_latents(jax.random.fold_in(streams_of[9], 71), 0)
    queries = draw_queries(jax.random.fold_in(streams_of[9], 71), 0)
    attn_keys = draw_attn_keys(jax.random.fold_in(streams_of[9], 71), 0)
    cached = gaussian(streams_of[3], (BLOCKS, WINDOWS, FRAMES, SPATIAL, D), 0.5, 3.0, ((1, 32), (3, 8)))
    plan = draw_plan(jax.random.fold_in(streams_of[9], 71), 0)
    refresh = draw_refresh(jax.random.fold_in(streams_of[9], 71), 0)
    value_gain = jnp.clip(1.0 + 0.18 * jax.random.normal(streams_of[6], (D,), jnp.float32), 0.1, 1.9)
    attn_gate = jnp.clip(jnp.exp(jax.random.uniform(streams_of[7], (D,), jnp.float32, math.log(0.5), math.log(3.0))), 0.5, 3.0)
    intersections = draw_intersections(jax.random.fold_in(streams_of[9], 71), 0)
    return {"latents": latents, "queries": queries, "attn_keys": attn_keys, "cached": cached, "plan": plan, "refresh": refresh, "value_gain": value_gain, "attn_gate": attn_gate, "intersections": intersections}


def attend(query_win, key_win, value_win):
    rows = FRAMES * SPATIAL
    inv_root = 1.0 / math.sqrt(HEAD_DIM)
    query_f = query_win.reshape(rows, HEADS, HEAD_DIM).astype(jnp.float32)
    key_f = key_win.reshape(rows, HEADS, HEAD_DIM).astype(jnp.float32)
    value_f = value_win.reshape(rows, HEADS, HEAD_DIM).astype(jnp.float32)
    scores = jnp.einsum('qhd,khd->hqk', query_f, key_f) * inv_root
    peak = lax.optimization_barrier(jnp.max(scores, axis=-1, keepdims=True))
    weights = jnp.exp(scores - peak)
    summed = lax.optimization_barrier(jnp.sum(weights, axis=-1))
    rounded = lax.optimization_barrier(weights.astype(jnp.bfloat16)).astype(jnp.float32)
    mixed = jnp.einsum('hqk,khd->qhd', rounded, value_f) / jnp.transpose(summed)[:, :, None]
    return mixed.astype(jnp.bfloat16).reshape(FRAMES, SPATIAL, D)

def reference(latents, queries, attn_keys, cached, plan, refresh, value_gain, attn_gate, intersections):
    block_ids = jnp.arange(BLOCKS, dtype=jnp.int32)
    sched_f = plan.astype(jnp.float32)

    def window_step(widx):
        chosen = lax.dynamic_index_in_dim(refresh, widx, 0, keepdims=False)
        mix_before = jnp.where(block_ids < chosen, sched_f, jnp.float32(0.0))
        mix_after = jnp.where(block_ids > chosen, sched_f, jnp.float32(0.0))
        own = lax.dynamic_index_in_dim(latents, widx, 0, keepdims=False)
        stack = lax.dynamic_index_in_dim(cached, widx, 1, keepdims=False)
        query_win = lax.dynamic_index_in_dim(queries, widx, 0, keepdims=False)
        key_win = lax.dynamic_index_in_dim(attn_keys, widx, 0, keepdims=False)
        hidden = own.astype(jnp.float32)
        for block in range(BLOCKS):
            hidden = hidden + mix_before[block] * stack[block].astype(jnp.float32)
        mean_square = lax.optimization_barrier(jnp.mean(hidden * hidden, axis=-1, keepdims=True))
        values = lax.optimization_barrier((hidden / jnp.sqrt(mean_square + 1e-06) * value_gain).astype(jnp.bfloat16))
        attended = lax.optimization_barrier(attend(query_win, key_win, values))
        later = hidden
        for block in range(BLOCKS):
            later = later + mix_after[block] * stack[block].astype(jnp.float32)
        return (later + attn_gate * attended.astype(jnp.float32)).astype(jnp.bfloat16)
    window_ids = jnp.arange(WINDOWS, dtype=jnp.int32)
    pre = lax.optimization_barrier(lax.map(window_step, window_ids))

    def blend(widx):
        prev_w = (widx + WINDOWS - 1) % WINDOWS
        next_w = (widx + 1) % WINDOWS
        mine = lax.dynamic_index_in_dim(pre, widx, 0, keepdims=False).astype(jnp.float32)
        before_win = lax.dynamic_index_in_dim(pre, prev_w, 0, keepdims=False)
        after_win = lax.dynamic_index_in_dim(pre, next_w, 0, keepdims=False)
        ov_next = intersections[widx]
        ov_prev = intersections[prev_w]
        frame_ids = jnp.arange(FRAMES, dtype=jnp.int32)
        tail_pos = frame_ids - (FRAMES - ov_next)
        in_tail = (tail_pos >= 0)[:, None, None]
        in_head = (frame_ids < ov_prev)[:, None, None]
        next_idx = jnp.clip(tail_pos, 0, FRAMES - 1).astype(jnp.int32)
        prev_idx = jnp.clip(FRAMES - ov_prev + frame_ids, 0, FRAMES - 1).astype(jnp.int32)
        partner_next = jnp.take(after_win, next_idx, axis=0).astype(jnp.float32)
        partner_prev = jnp.take(before_win, prev_idx, axis=0).astype(jnp.float32)
        ramp_tail = ((tail_pos + 1).astype(jnp.float32) / (ov_next + 1).astype(jnp.float32))[:, None, None]
        ramp_head = ((frame_ids + 1).astype(jnp.float32) / (ov_prev + 1).astype(jnp.float32))[:, None, None]
        tail_mix = (1.0 - ramp_tail) * mine + ramp_tail * partner_next
        head_mix = (1.0 - ramp_head) * partner_prev + ramp_head * mine
        return jnp.where(in_tail, tail_mix, jnp.where(in_head, head_mix, mine)).astype(jnp.bfloat16)
    return lax.map(blend, window_ids)
```

```python
import math

import jax
import jax.numpy as jnp
from jax import lax
from jax.experimental import pallas as pl
from jax.experimental.pallas import tpu as pltpu
from jax.sharding import PartitionSpec as P

HEAD_DIM = 128
MAXOV = 4
XS, YS = 2, 4
MOVES = (0, 1, 3, 2)
ANY = pl.BlockSpec(memory_space=pl.ANY)
SMEM = pl.BlockSpec(memory_space=pltpu.SMEM)
VMEM_BYTES = 56 * 2**20
PARTS = (6, 4)


def send(value, move):
    pairs = [(x * YS + y, x * YS + (y + move) % YS) for x in range(XS) for y in range(YS)]
    return lax.ppermute(value, "token", pairs)


def send_back(value, move):
    return send(value, YS - move)


def across(value):
    half = XS // 2
    pairs = [(x * YS + y, (x + half) % XS * YS + y) for x in range(XS) for y in range(YS)]
    return lax.ppermute(value, "token", pairs)


def owner(move):
    return lax.rem(lax.axis_index("token") + move, YS)


def lanes(start, size):
    return pl.ds(pl.multiple_of(start, HEAD_DIM), size)


def whole(refs, sems):
    copies = [pltpu.make_async_copy(a, b, sems.at[i]) for i, (a, b) in enumerate(refs)]
    for copy in copies:
        copy.start()
    return copies


def pack(value, wide, after=()):
    rows = value.shape[0]
    count = len(MOVES)

    def body(value_ref, *refs):
        refs = refs[len(after) :]
        outs, (held, in_sems, out_sems) = refs[:count], refs[count:]
        arriving = whole(
            [
                (value_ref.at[:, lanes(owner(move) * wide, wide)], held.at[i])
                for i, move in enumerate(MOVES)
            ],
            in_sems,
        )
        leaving = [
            pltpu.make_async_copy(held.at[i], outs[i], out_sems.at[i]) for i in range(count)
        ]
        for i in range(count):
            arriving[i].wait()
            leaving[i].start()
        for copy in leaving:
            copy.wait()

    return pl.pallas_call(
        body,
        name="pack",
        out_shape=[jax.ShapeDtypeStruct((rows, wide), value.dtype)] * count,
        in_specs=[ANY] * (1 + len(after)),
        out_specs=[ANY] * count,
        scratch_shapes=[
            pltpu.VMEM((count, rows, wide), value.dtype),
            pltpu.SemaphoreType.DMA((count,)),
            pltpu.SemaphoreType.DMA((count,)),
        ],
        compiler_params=pltpu.CompilerParams(vmem_limit_bytes=4 * 2**20),
        cost_estimate=pl.CostEstimate(flops=0, bytes_accessed=4 * value.size, transcendentals=0),
    )(value, *after)


def stack(pieces, skip, take, after=()):
    rows = pieces[0].shape[0]
    count = len(pieces)

    def body(*refs):
        sources = refs[:count]
        out, held, in_sems, out_sem = refs[count + len(after) :]
        arriving = whole(
            [
                (source.at[:, pl.ds(skip, take)], held.at[pl.ds(i * rows, rows)])
                for i, source in enumerate(sources)
            ],
            in_sems,
        )
        for copy in arriving:
            copy.wait()
        leaving = pltpu.make_async_copy(held, out, out_sem)
        leaving.start()
        leaving.wait()

    return pl.pallas_call(
        body,
        name="stack",
        out_shape=jax.ShapeDtypeStruct((count * rows, take), pieces[0].dtype),
        in_specs=[ANY] * (count + len(after)),
        out_specs=ANY,
        scratch_shapes=[
            pltpu.VMEM((count * rows, take), pieces[0].dtype),
            pltpu.SemaphoreType.DMA((count,)),
            pltpu.SemaphoreType.DMA,
        ],
        compiler_params=pltpu.CompilerParams(vmem_limit_bytes=4 * 2**20),
        cost_estimate=pl.CostEstimate(
            flops=0, bytes_accessed=4 * count * rows * take, transcendentals=0
        ),
    )(*pieces, *after)


def hide(latents, cached, plan, refresh, gain, wide, parts, after):
    blocks = cached.shape[0]
    frames, spots, width = latents.shape
    count = len(MOVES)
    step = 3
    rows = step * spots

    def body(plan_ref, refresh_ref, latents_ref, cached_ref, gain_ref, *refs):
        values_ref, *laters, later_ref = refs[1:]
        chosen = refresh_ref[lax.axis_index("window")]
        for i in range(step):
            span = pl.ds(i * spots, spots)
            hidden = latents_ref[i].astype(jnp.float32)
            after = jnp.zeros_like(hidden)
            for b in range(blocks):
                mix = plan_ref[b].astype(jnp.float32)
                block = cached_ref[b, i].astype(jnp.float32)
                hidden = hidden + jnp.where(b < chosen, mix, 0.0) * block
                after = after + jnp.where(b > chosen, mix, 0.0) * block
            later_ref[span, :] = hidden + after
            mean_square = jnp.mean(hidden * hidden, axis=-1, keepdims=True)
            values = hidden * lax.rsqrt(mean_square + 1e-06) * gain_ref[...]
            values_ref[span, :] = values.astype(values_ref.dtype)
        for i, move in enumerate(MOVES):
            start = owner(move) * wide
            skip = 0
            for take, later in zip(parts, laters):
                later[:, pl.ds(i * take, take)] = later_ref[:, lanes(start + skip, take)]
                skip += take

    return pl.pallas_call(
        body,
        name="hide",
        grid=(frames // step,),
        out_shape=[jax.ShapeDtypeStruct((frames * spots, width), jnp.bfloat16)]
        + [jax.ShapeDtypeStruct((frames * spots, count * take), jnp.float32) for take in parts],
        in_specs=[
            SMEM,
            SMEM,
            pl.BlockSpec((step, spots, width), lambda f: (f, 0, 0)),
            pl.BlockSpec((blocks, step, spots, width), lambda f: (0, f, 0, 0)),
            pl.BlockSpec((1, width), lambda f: (0, 0)),
            ANY,
        ],
        out_specs=[pl.BlockSpec((rows, width), lambda f: (f, 0))]
        + [pl.BlockSpec((rows, count * take), lambda f: (f, 0)) for take in parts],
        scratch_shapes=[pltpu.VMEM((rows, width), jnp.float32)],
        compiler_params=pltpu.CompilerParams(vmem_limit_bytes=VMEM_BYTES),
        cost_estimate=pl.CostEstimate(
            flops=20 * latents.size, bytes_accessed=16 * latents.size, transcendentals=0
        ),
    )(plan, refresh, latents, cached, gain, after)


def attend(asked, keys, values, skip, take):
    rows = asked[0].shape[0]
    count, places = len(asked), len(keys)
    pieces = [(piece, 0, skip) for piece in asked] + keys + values
    arrays = list({id(piece[0]): piece[0] for piece in pieces}.values())
    index = {id(array): i for i, array in enumerate(arrays)}
    where = [(index[id(array)], row, col) for array, row, col in pieces]
    block = count * rows // 2
    scale = math.log2(math.e) / math.sqrt(HEAD_DIM)

    def body(*refs):
        sources, outs = refs[: len(arrays)], refs[len(arrays) : len(arrays) + count]
        q_ref, k_ref, v_ref, result, in_sems, out_sems = refs[len(arrays) + count :]
        holds = (
            [q_ref.at[pl.ds(i * rows, rows)] for i in range(count)]
            + [k_ref.at[pl.ds(i * rows, rows)] for i in range(places)]
            + [v_ref.at[pl.ds(i * rows, rows)] for i in range(places)]
        )
        arriving = whole(
            [
                (sources[i].at[pl.ds(row, rows), pl.ds(col, take)], held)
                for (i, row, col), held in zip(where, holds)
            ],
            in_sems,
        )
        for copy in arriving:
            copy.wait()

        @pl.loop(0, take // HEAD_DIM)
        def _(head):
            cols = lanes(head * HEAD_DIM, HEAD_DIM)
            for i in range(count * rows // block):
                span = pl.ds(i * block, block)
                scores = lax.dot_general(
                    q_ref[span, cols],
                    k_ref[:, cols],
                    (((1,), (1,)), ((), ())),
                    preferred_element_type=jnp.float32,
                )
                peak = jnp.max(scores, axis=1, keepdims=True)
                weights = jnp.exp2((scores - peak) * scale).astype(jnp.bfloat16)
                value = v_ref[:, cols]
                both = jnp.concatenate([value, jnp.ones_like(value)], axis=1)
                total = jnp.dot(weights, both, preferred_element_type=jnp.float32)
                result[span, cols] = (total[:, :HEAD_DIM] / total[:, HEAD_DIM:]).astype(
                    result.dtype
                )

        leaving = whole(
            [(result.at[pl.ds(i * rows, rows)], out) for i, out in enumerate(outs)], out_sems
        )
        for copy in leaving:
            copy.wait()

    work = count * rows * places * rows * take
    return pl.pallas_call(
        body,
        name="attend",
        out_shape=[jax.ShapeDtypeStruct((rows, take), jnp.bfloat16)] * count,
        in_specs=[ANY] * len(arrays),
        out_specs=[ANY] * count,
        scratch_shapes=[
            pltpu.VMEM((count * rows, take), jnp.bfloat16),
            pltpu.VMEM((places * rows, take), jnp.bfloat16),
            pltpu.VMEM((places * rows, take), jnp.bfloat16),
            pltpu.VMEM((count * rows, take), jnp.bfloat16),
            pltpu.SemaphoreType.DMA((len(pieces),)),
            pltpu.SemaphoreType.DMA((count,)),
        ],
        compiler_params=pltpu.CompilerParams(vmem_limit_bytes=24 * 2**20),
        cost_estimate=pl.CostEstimate(
            flops=8 * work,
            bytes_accessed=12 * places * rows * take,
            transcendentals=work // HEAD_DIM,
        ),
    )(*arrays)


def join(later, gate, attended, frames, wide, skip):
    count = len(MOVES)
    rows, take = attended[0].shape
    spots = rows // frames
    ends = MAXOV * spots
    sizes = (ends, rows - 2 * ends, ends)

    def body(later_ref, gate_ref, *refs):
        pieces, outs = refs[:count], refs[count : count + 3]
        laters, held, result, in_sems, out_sems = refs[count + 3 :]
        arriving = []
        for i in range(count):
            span = pl.ds(i * take, take)
            arriving.append(
                pltpu.make_async_copy(later_ref.at[:, span], laters.at[:, span], in_sems.at[i, 0])
            )
            arriving.append(
                pltpu.make_async_copy(pieces[i], held.at[:, span], in_sems.at[i, 1])
            )
        for copy in arriving:
            copy.start()
        for i, move in enumerate(MOVES):
            span = pl.ds(i * take, take)
            gates = gate_ref[:, lanes(owner(move) * wide + skip, take)]
            arriving[2 * i].wait()
            arriving[2 * i + 1].wait()
            pre = laters[:, span] + gates * held[:, span].astype(jnp.float32)
            result[:, span] = pre.astype(result.dtype)
        leaving, start = [], 0
        for i, size in enumerate(sizes):
            leaving.append(
                pltpu.make_async_copy(result.at[pl.ds(start, size)], outs[i], out_sems.at[i])
            )
            start += size
        for copy in leaving:
            copy.start()
        for copy in leaving:
            copy.wait()

    return pl.pallas_call(
        body,
        name="join",
        out_shape=[jax.ShapeDtypeStruct((size, count * take), jnp.bfloat16) for size in sizes],
        in_specs=[ANY, pl.BlockSpec(memory_space=pltpu.VMEM)] + [ANY] * count,
        out_specs=[ANY] * 3,
        scratch_shapes=[
            pltpu.VMEM((rows, count * take), jnp.float32),
            pltpu.VMEM((rows, count * take), jnp.bfloat16),
            pltpu.VMEM((rows, count * take), jnp.bfloat16),
            pltpu.SemaphoreType.DMA((count, 2)),
            pltpu.SemaphoreType.DMA((3,)),
        ],
        compiler_params=pltpu.CompilerParams(vmem_limit_bytes=8 * 2**20),
        cost_estimate=pl.CostEstimate(
            flops=2 * later.size, bytes_accessed=8 * later.size, transcendentals=0
        ),
    )(later, gate, *attended)


def blend(intersections, first, middle, last, from_prev, from_next, frames, wide, skip, before):
    count = len(MOVES)
    take = first.shape[1] // count
    ends = first.shape[0]
    spots = ends // MAXOV
    rows = frames * spots

    def body(overlaps_ref, *refs):
        sources = refs[:5]
        out_ref, result, mine, prev, after, in_sems, out_sems = refs[-7:]
        window, windows = lax.axis_index("window"), lax.axis_size("window")
        ov_next = overlaps_ref[window]
        ov_prev = overlaps_ref[lax.rem(window + windows - 1, windows)]
        first_in, last_in = mine.at[pl.ds(0, ends)], mine.at[pl.ds(ends, ends)]
        middle_in = result.at[pl.ds(ends, rows - 2 * ends)]
        arriving = whole(
            zip(sources, (first_in, middle_in, last_in, prev, after)), in_sems
        )
        for copy in arriving:
            copy.wait()
        for f in range(MAXOV):
            ramp = jnp.where(
                f < ov_prev, jnp.float32(f + 1) / (ov_prev + 1).astype(jnp.float32), 1.0
            )
            other = jnp.clip(MAXOV - ov_prev + f, 0, MAXOV - 1) * spots
            mixed = (1.0 - ramp) * prev[pl.ds(pl.multiple_of(other, 16), spots), :].astype(
                jnp.float32
            ) + ramp * mine[pl.ds(f * spots, spots), :].astype(jnp.float32)
            result[pl.ds(f * spots, spots), :] = mixed.astype(result.dtype)
        for f in range(frames - MAXOV, frames):
            tail = f - frames + ov_next
            ramp = jnp.where(
                tail >= 0,
                (tail + 1).astype(jnp.float32) / (ov_next + 1).astype(jnp.float32),
                0.0,
            )
            other = jnp.clip(tail, 0, MAXOV - 1) * spots
            own = pl.ds(ends + (f - frames + MAXOV) * spots, spots)
            mixed = (1.0 - ramp) * mine[own, :].astype(jnp.float32) + ramp * after[
                pl.ds(pl.multiple_of(other, 16), spots), :
            ].astype(jnp.float32)
            result[pl.ds(f * spots, spots), :] = mixed.astype(result.dtype)
        leaving = whole(
            [
                (
                    result.at[:, pl.ds(i * take, take)],
                    out_ref.at[:, lanes(owner(move) * wide + skip, take)],
                )
                for i, move in enumerate(MOVES)
            ],
            out_sems,
        )
        for copy in leaving:
            copy.wait()

    extra = () if before is None else (before,)
    return pl.pallas_call(
        body,
        name="blend",
        out_shape=jax.ShapeDtypeStruct((rows, count * wide), jnp.bfloat16),
        in_specs=[SMEM] + [ANY] * (5 + len(extra)),
        out_specs=ANY,
        input_output_aliases={6: 0} if extra else {},
        scratch_shapes=[
            pltpu.VMEM((rows, count * take), jnp.bfloat16),
            pltpu.VMEM((2 * ends, count * take), jnp.bfloat16),
            pltpu.VMEM((ends, count * take), jnp.bfloat16),
            pltpu.VMEM((ends, count * take), jnp.bfloat16),
            pltpu.SemaphoreType.DMA((5,)),
            pltpu.SemaphoreType.DMA((count,)),
        ],
        compiler_params=pltpu.CompilerParams(vmem_limit_bytes=6 * 2**20),
        cost_estimate=pl.CostEstimate(
            flops=4 * rows * count * take,
            bytes_accessed=8 * rows * count * take,
            transcendentals=0,
        ),
    )(intersections, first, middle, last, from_prev, from_next, *extra)


def shift(value, steps):
    count = lax.axis_size("window")
    pairs = [(source, (source + steps) % count) for source in range(count)]
    return lax.ppermute(value, "window", pairs)


def spread(pieces, how):
    return [how(piece, move) if move else piece for piece, move in zip(pieces, MOVES)]


def on_device(
    latents, queries, attn_keys, cached, plan, refresh, value_gain, attn_gate, intersections
):
    _, frames, spots, width = latents.shape
    rows = frames * spots
    wide = width // len(MOVES)
    parts = [heads * HEAD_DIM for heads in PARTS]
    skips = [sum(parts[:i]) for i in range(len(parts))]
    queries = queries.reshape(rows, width)
    gate = attn_gate.reshape(1, width)
    packed = pack(attn_keys.reshape(rows, width), wide)
    keys = spread(packed, send)
    values, *laters = hide(
        latents[0],
        cached[:, 0],
        plan,
        refresh,
        value_gain.reshape(1, width),
        wide,
        parts,
        packed[0],
    )
    far_keys = [across(key) for key in keys[:3]]
    values = spread(pack(values, wide, (*keys[1:3], far_keys[0])), send)
    far_value = across(values[0])
    asked = spread(pack(queries, wide, (*values[1:3], far_keys[1])), send)
    moved = [keys[3], *values[1:]]
    afters = ((far_keys[1], far_value), (far_keys[2],))
    rests = [
        across(stack(moved, skip, take, after))
        for skip, take, after in zip(skips, parts, afters)
    ]
    out = None
    for later, rest, skip, take in zip(laters, rests, skips, parts):
        key_places = [(key, 0, skip) for key in keys + far_keys] + [(rest, 0, 0)]
        value_places = [(value, 0, skip) for value in [*values, far_value]] + [
            (rest, i * rows, 0) for i in (1, 2, 3)
        ]
        attended = spread(attend(asked, key_places, value_places, skip, take), send_back)
        first, middle, last = join(later, gate, attended, frames, wide, skip)
        from_prev = shift(last, 1)
        from_next = shift(first, -1)
        out = blend(
            intersections, first, middle, last, from_prev, from_next, frames, wide, skip, out
        )
    return out.reshape(1, frames, spots, width)


def solution(mesh):
    in_specs = (
        P("window", None, "token", None),
        P("window", None, "token", None),
        P("window", None, "token", None),
        P(None, "window", None, "token", None),
        P(),
        P(),
        P(),
        P(),
        P(),
    )
    out_specs = P("window", None, "token", None)
    return jax.shard_map(
        on_device, mesh=mesh, in_specs=in_specs, out_specs=out_specs, check_vma=False
    )
```

```python
import math

import jax
import jax.numpy as jnp
from jax import lax
from jax.experimental import pallas as pl
from jax.experimental.pallas import tpu as pltpu
from jax.sharding import PartitionSpec as P

HEAD_DIM = 128
MAXOV = 4
XS, YS = 2, 4
MOVES = (0, 1, 3, 2)
ANY = pl.BlockSpec(memory_space=pl.ANY)
SMEM = pl.BlockSpec(memory_space=pltpu.SMEM)
VMEM = pl.BlockSpec(memory_space=pltpu.VMEM)
VMEM_BYTES = 56 * 2**20
PARTS = (6, 4)


def send(value, move):
    pairs = [(x * YS + y, x * YS + (y + move) % YS) for x in range(XS) for y in range(YS)]
    return lax.ppermute(value, "token", pairs)


def send_back(value, move):
    return send(value, YS - move)


def across(value):
    half = XS // 2
    pairs = [(x * YS + y, (x + half) % XS * YS + y) for x in range(XS) for y in range(YS)]
    return lax.ppermute(value, "token", pairs)


def owner(move):
    return lax.rem(lax.axis_index("token") + move, YS)


def lanes(start, size):
    return pl.ds(pl.multiple_of(start, HEAD_DIM), size)


def whole(refs, sems):
    copies = [pltpu.make_async_copy(a, b, sems.at[i]) for i, (a, b) in enumerate(refs)]
    for copy in copies:
        copy.start()
    return copies


def pack(value, wide, moves, after=()):
    rows = value.shape[0]
    count = len(moves)

    def body(value_ref, *refs):
        outs, sems = refs[len(after) : -1], refs[-1]
        copies = whole(
            [
                (value_ref.at[:, lanes(owner(move) * wide, wide)], out)
                for move, out in zip(moves, outs)
            ],
            sems,
        )
        for copy in copies:
            copy.wait()

    return pl.pallas_call(
        body,
        name="pack",
        out_shape=[jax.ShapeDtypeStruct((rows, wide), value.dtype)] * count,
        in_specs=[ANY] * (1 + len(after)),
        out_specs=[VMEM] * count,
        scratch_shapes=[pltpu.SemaphoreType.DMA((count,))],
        compiler_params=pltpu.CompilerParams(vmem_limit_bytes=4 * 2**20),
        cost_estimate=pl.CostEstimate(
            flops=0, bytes_accessed=4 * count * rows * wide, transcendentals=0
        ),
    )(value, *after)


def stack(pieces, skip, take, after=()):
    rows = pieces[0].shape[0]
    count = len(pieces)

    def body(*refs):
        sources = refs[:count]
        out, held, in_sems, out_sem = refs[count + len(after) :]
        arriving = whole(
            [
                (source.at[:, pl.ds(skip, take)], held.at[pl.ds(i * rows, rows)])
                for i, source in enumerate(sources)
            ],
            in_sems,
        )
        for copy in arriving:
            copy.wait()
        leaving = pltpu.make_async_copy(held, out, out_sem)
        leaving.start()
        leaving.wait()

    return pl.pallas_call(
        body,
        name="stack",
        out_shape=jax.ShapeDtypeStruct((count * rows, take), pieces[0].dtype),
        in_specs=[ANY] * (count + len(after)),
        out_specs=ANY,
        scratch_shapes=[
            pltpu.VMEM((count * rows, take), pieces[0].dtype),
            pltpu.SemaphoreType.DMA((count,)),
            pltpu.SemaphoreType.DMA,
        ],
        compiler_params=pltpu.CompilerParams(vmem_limit_bytes=4 * 2**20),
        cost_estimate=pl.CostEstimate(
            flops=0, bytes_accessed=4 * count * rows * take, transcendentals=0
        ),
    )(*pieces, *after)


def hold(values, after):
    count = len(values)

    def body(*refs):
        del refs

    return pl.pallas_call(
        body,
        name="hold",
        out_shape=[jax.ShapeDtypeStruct(value.shape, value.dtype) for value in values],
        in_specs=[ANY] * (count + len(after)),
        out_specs=[ANY] * count,
        input_output_aliases={i: i for i in range(count)},
        compiler_params=pltpu.CompilerParams(vmem_limit_bytes=2**20),
    )(*values, *after)


def mixes(plan_ref, refresh_ref, blocks):
    chosen = refresh_ref[lax.axis_index("window")]
    plan = [plan_ref[b].astype(jnp.float32) for b in range(blocks)]
    before = [jnp.where(b < chosen, plan[b], 0.0) for b in range(blocks)]
    after = [jnp.where(b > chosen, plan[b], 0.0) for b in range(blocks)]
    return before, after


def prepare(latents, cached, plan, refresh, gain, wide, after):
    blocks = cached.shape[0]
    frames, spots, width = latents.shape
    count = len(MOVES)
    step = 3
    rows = step * spots

    def body(plan_ref, refresh_ref, latents_ref, cached_ref, gain_ref, *refs):
        outs, values_ref = refs[len(after) : -1], refs[-1]
        before, _ = mixes(plan_ref, refresh_ref, blocks)
        for i in range(step):
            hidden = latents_ref[i].astype(jnp.float32)
            for b in range(blocks):
                hidden = hidden + before[b] * cached_ref[b, i].astype(jnp.float32)
            mean_square = jnp.mean(hidden * hidden, axis=-1, keepdims=True)
            values = hidden * lax.rsqrt(mean_square + 1e-06) * gain_ref[...]
            values_ref[pl.ds(i * spots, spots), :] = values.astype(values_ref.dtype)
        for move, out in zip(MOVES, outs):
            out[...] = values_ref[:, lanes(owner(move) * wide, wide)]

    return pl.pallas_call(
        body,
        name="prepare",
        grid=(frames // step,),
        out_shape=[jax.ShapeDtypeStruct((frames * spots, wide), jnp.bfloat16)] * count,
        in_specs=[
            SMEM,
            SMEM,
            pl.BlockSpec((step, spots, width), lambda f: (f, 0, 0)),
            pl.BlockSpec((blocks, step, spots, width), lambda f: (0, f, 0, 0)),
            pl.BlockSpec((1, width), lambda f: (0, 0)),
        ]
        + [ANY] * len(after),
        out_specs=[pl.BlockSpec((rows, wide), lambda f: (f, 0))] * count,
        scratch_shapes=[pltpu.VMEM((rows, width), jnp.bfloat16)],
        compiler_params=pltpu.CompilerParams(vmem_limit_bytes=16 * 2**20),
        cost_estimate=pl.CostEstimate(
            flops=20 * latents.size, bytes_accessed=12 * latents.size, transcendentals=0
        ),
    )(plan, refresh, latents, cached, gain, *after)


def add(latents, cached, plan, refresh, wide, parts):
    blocks = cached.shape[0]
    frames, spots, width = latents.shape
    count = len(MOVES)
    step = 3
    rows = step * spots

    def body(plan_ref, refresh_ref, latents_ref, cached_ref, *refs):
        laters, later_ref = refs[:-1], refs[-1]
        before, after = mixes(plan_ref, refresh_ref, blocks)
        for i in range(step):
            later = latents_ref[i].astype(jnp.float32)
            for b in range(blocks):
                later = later + (before[b] + after[b]) * cached_ref[b, i].astype(jnp.float32)
            later_ref[pl.ds(i * spots, spots), :] = later
        for i, move in enumerate(MOVES):
            start = owner(move) * wide
            for take, later in zip(parts, laters):
                later[:, pl.ds(i * take, take)] = later_ref[:, lanes(start, take)]
                start += take

    return pl.pallas_call(
        body,
        name="add",
        grid=(frames // step,),
        out_shape=[
            jax.ShapeDtypeStruct((frames * spots, count * take), jnp.float32) for take in parts
        ],
        in_specs=[
            SMEM,
            SMEM,
            pl.BlockSpec((step, spots, width), lambda f: (f, 0, 0)),
            pl.BlockSpec((blocks, step, spots, width), lambda f: (0, f, 0, 0)),
        ],
        out_specs=[pl.BlockSpec((rows, count * take), lambda f: (f, 0)) for take in parts],
        scratch_shapes=[pltpu.VMEM((rows, width), jnp.float32)],
        compiler_params=pltpu.CompilerParams(vmem_limit_bytes=24 * 2**20),
        cost_estimate=pl.CostEstimate(
            flops=10 * latents.size, bytes_accessed=14 * latents.size, transcendentals=0
        ),
    )(plan, refresh, latents, cached)


def attend(asked, keys, values, skip, take):
    rows = asked[0].shape[0]
    count, places = len(asked), len(keys)
    pieces = [(piece, 0, skip) for piece in asked] + keys + values
    arrays = list({id(piece[0]): piece[0] for piece in pieces}.values())
    index = {id(array): i for i, array in enumerate(arrays)}
    where = [(index[id(array)], row, col) for array, row, col in pieces]
    scale = math.log2(math.e) / math.sqrt(HEAD_DIM)
    unroll = 2

    def body(*refs):
        sources, outs = refs[: len(arrays)], refs[len(arrays) :]

        def rows_of(chosen, first):
            return jnp.concatenate(
                [
                    sources[i][pl.ds(row, rows), lanes(col + first, HEAD_DIM)]
                    for i, row, col in chosen
                ],
                axis=0,
            )

        @pl.loop(0, take // (unroll * HEAD_DIM))
        def _(step):
            for u in range(unroll):
                first = (step * unroll + u) * HEAD_DIM
                query = rows_of(where[:count], first)
                key = rows_of(where[count : count + places], first)
                value = rows_of(where[count + places :], first)
                scores = lax.dot_general(
                    query, key, (((1,), (1,)), ((), ())), preferred_element_type=jnp.float32
                )
                peak = jnp.max(scores, axis=1, keepdims=True)
                weights = jnp.exp2((scores - peak) * scale).astype(jnp.bfloat16)
                both = jnp.concatenate([value, jnp.ones_like(value)], axis=1)
                total = jnp.dot(weights, both, preferred_element_type=jnp.float32)
                result = (total[:, :HEAD_DIM] / total[:, HEAD_DIM:]).astype(jnp.bfloat16)
                for i, out in enumerate(outs):
                    out[:, lanes(first, HEAD_DIM)] = result[i * rows : (i + 1) * rows]

    work = count * rows * places * rows * take
    return pl.pallas_call(
        body,
        name="attend",
        out_shape=[jax.ShapeDtypeStruct((rows, take), jnp.bfloat16)] * count,
        in_specs=[VMEM] * len(arrays),
        out_specs=[VMEM] * count,
        compiler_params=pltpu.CompilerParams(vmem_limit_bytes=24 * 2**20),
        cost_estimate=pl.CostEstimate(
            flops=8 * work,
            bytes_accessed=12 * places * rows * take,
            transcendentals=work // HEAD_DIM,
        ),
    )(*arrays)


def join(later, gate, attended, frames, wide, skip):
    count = len(MOVES)
    rows, take = attended[0].shape
    spots = rows // frames
    ends = MAXOV * spots
    sizes = (ends, rows - 2 * ends, ends)

    def body(later_ref, gate_ref, *refs):
        pieces, outs = refs[:count], refs[count:]
        for i, move in enumerate(MOVES):
            span = pl.ds(i * take, take)
            gates = gate_ref[:, lanes(owner(move) * wide + skip, take)]
            pre = later_ref[:, span] + gates * pieces[i][...].astype(jnp.float32)
            pre, start = pre.astype(jnp.bfloat16), 0
            for out, size in zip(outs, sizes):
                out[:, span] = pre[start : start + size]
                start += size

    return pl.pallas_call(
        body,
        name="join",
        out_shape=[jax.ShapeDtypeStruct((size, count * take), jnp.bfloat16) for size in sizes],
        in_specs=[VMEM] * (2 + count),
        out_specs=[VMEM] * 3,
        compiler_params=pltpu.CompilerParams(vmem_limit_bytes=8 * 2**20),
        cost_estimate=pl.CostEstimate(
            flops=2 * later.size, bytes_accessed=8 * later.size, transcendentals=0
        ),
    )(later, gate, *attended)


def blend(intersections, first, middle, last, from_prev, from_next, frames, wide, skip, before):
    count = len(MOVES)
    take = first.shape[1] // count
    ends = first.shape[0]
    spots = ends // MAXOV
    rows = frames * spots

    def body(overlaps_ref, *refs):
        first_ref, middle_ref, last_ref, prev, after = refs[:5]
        out_ref, result, out_sems = refs[-3:]
        window, windows = lax.axis_index("window"), lax.axis_size("window")
        ov_next = overlaps_ref[window]
        ov_prev = overlaps_ref[lax.rem(window + windows - 1, windows)]
        result[pl.ds(ends, rows - 2 * ends), :] = middle_ref[...]
        for f in range(MAXOV):
            ramp = jnp.where(
                f < ov_prev, jnp.float32(f + 1) / (ov_prev + 1).astype(jnp.float32), 1.0
            )
            other = jnp.clip(MAXOV - ov_prev + f, 0, MAXOV - 1) * spots
            mixed = (1.0 - ramp) * prev[pl.ds(pl.multiple_of(other, 16), spots), :].astype(
                jnp.float32
            ) + ramp * first_ref[pl.ds(f * spots, spots), :].astype(jnp.float32)
            result[pl.ds(f * spots, spots), :] = mixed.astype(result.dtype)
        for f in range(frames - MAXOV, frames):
            tail = f - frames + ov_next
            ramp = jnp.where(
                tail >= 0,
                (tail + 1).astype(jnp.float32) / (ov_next + 1).astype(jnp.float32),
                0.0,
            )
            other = jnp.clip(tail, 0, MAXOV - 1) * spots
            own = pl.ds((f - frames + MAXOV) * spots, spots)
            mixed = (1.0 - ramp) * last_ref[own, :].astype(jnp.float32) + ramp * after[
                pl.ds(pl.multiple_of(other, 16), spots), :
            ].astype(jnp.float32)
            result[pl.ds(f * spots, spots), :] = mixed.astype(result.dtype)
        leaving = whole(
            [
                (
                    result.at[:, pl.ds(i * take, take)],
                    out_ref.at[:, lanes(owner(move) * wide + skip, take)],
                )
                for i, move in enumerate(MOVES)
            ],
            out_sems,
        )
        for copy in leaving:
            copy.wait()

    extra = () if before is None else (before,)
    return pl.pallas_call(
        body,
        name="blend",
        out_shape=jax.ShapeDtypeStruct((rows, count * wide), jnp.bfloat16),
        in_specs=[SMEM] + [VMEM] * 5 + [ANY] * len(extra),
        out_specs=ANY,
        input_output_aliases={6: 0} if extra else {},
        scratch_shapes=[
            pltpu.VMEM((rows, count * take), jnp.bfloat16),
            pltpu.SemaphoreType.DMA((count,)),
        ],
        compiler_params=pltpu.CompilerParams(vmem_limit_bytes=6 * 2**20),
        cost_estimate=pl.CostEstimate(
            flops=4 * rows * count * take,
            bytes_accessed=8 * rows * count * take,
            transcendentals=0,
        ),
    )(intersections, first, middle, last, from_prev, from_next, *extra)


def shift(value, steps):
    count = lax.axis_size("window")
    pairs = [(source, (source + steps) % count) for source in range(count)]
    return lax.ppermute(value, "window", pairs)


def spread(pieces, how):
    return [how(piece, move) if move else piece for piece, move in zip(pieces, MOVES)]


def on_device(
    latents, queries, attn_keys, cached, plan, refresh, value_gain, attn_gate, intersections
):
    _, frames, spots, width = latents.shape
    rows = frames * spots
    wide = width // len(MOVES)
    parts = [heads * HEAD_DIM for heads in PARTS]
    skips = [sum(parts[:i]) for i in range(len(parts))]
    queries = queries.reshape(rows, width)
    gate = attn_gate.reshape(1, width)
    latents, cached = latents[0], cached[:, 0]
    attn_keys = attn_keys.reshape(rows, width)
    packed = pack(attn_keys, wide, MOVES)
    value, *values = prepare(
        latents, cached, plan, refresh, value_gain.reshape(1, width), wide, packed[:1]
    )
    far_keys = [across(packed[0])]
    keys = spread(packed, send)
    keys[1:3] = hold(keys[1:3], (value,))
    far_value = across(value)
    far_keys += [across(key) for key in keys[1:3]]
    near = hold(values[:2], (*keys[1:3], far_keys[0]))
    values = spread([value, *near, *hold(values[2:], (keys[3], far_value))], send)
    asked = spread(pack(queries, wide, MOVES, (*values[1:3], far_keys[1])), send)
    laters = add(latents, cached, plan, refresh, wide, parts)
    moved = [keys[3], *values[1:]]
    afters = ((*far_keys[1:], far_value, *laters), ())
    rests = [
        across(stack(moved, skip, take, after))
        for skip, take, after in zip(skips, parts, afters)
    ]
    out = None
    for later, rest, skip, take in zip(laters, rests, skips, parts):
        key_places = [(key, 0, skip) for key in keys + far_keys] + [(rest, 0, 0)]
        value_places = [(value, 0, skip) for value in [*values, far_value]] + [
            (rest, i * rows, 0) for i in (1, 2, 3)
        ]
        attended = spread(attend(asked, key_places, value_places, skip, take), send_back)
        first, middle, last = join(later, gate, attended, frames, wide, skip)
        from_prev = shift(last, 1)
        from_next = shift(first, -1)
        out = blend(
            intersections, first, middle, last, from_prev, from_next, frames, wide, skip, out
        )
    return out.reshape(1, frames, spots, width)


def solution(mesh):
    in_specs = (
        P("window", None, "token", None),
        P("window", None, "token", None),
        P("window", None, "token", None),
        P(None, "window", None, "token", None),
        P(),
        P(),
        P(),
        P(),
        P(),
    )
    out_specs = P("window", None, "token", None)
    return jax.shard_map(
        on_device, mesh=mesh, in_specs=in_specs, out_specs=out_specs, check_vma=False
    )
```

```python
import math

import jax
import jax.numpy as jnp
from jax import lax
from jax.experimental import pallas as pl
from jax.experimental.pallas import tpu as pltpu
from jax.sharding import PartitionSpec as P

HEAD_DIM = 128
MAXOV = 4
XS, YS = 2, 4
MOVES = (0, 1, 3, 2)
ANY = pl.BlockSpec(memory_space=pl.ANY)
SMEM = pl.BlockSpec(memory_space=pltpu.SMEM)
VMEM = pl.BlockSpec(memory_space=pltpu.VMEM)
VMEM_BYTES = 56 * 2**20
PARTS = (6, 4)


def send(value, move):
    pairs = [(x * YS + y, x * YS + (y + move) % YS) for x in range(XS) for y in range(YS)]
    return lax.ppermute(value, "token", pairs)


def send_back(value, move):
    return send(value, YS - move)


def across(value):
    half = XS // 2
    pairs = [(x * YS + y, (x + half) % XS * YS + y) for x in range(XS) for y in range(YS)]
    return lax.ppermute(value, "token", pairs)


def owner(move):
    return lax.rem(lax.axis_index("token") + move, YS)


def lanes(start, size):
    return pl.ds(pl.multiple_of(start, HEAD_DIM), size)


def whole(refs, sems):
    copies = [pltpu.make_async_copy(a, b, sems.at[i]) for i, (a, b) in enumerate(refs)]
    for copy in copies:
        copy.start()
    return copies


def pack(value, wide, moves, after=()):
    rows = value.shape[0]
    count = len(moves)

    def body(value_ref, *refs):
        outs, sems = refs[len(after) : -1], refs[-1]
        copies = whole(
            [
                (value_ref.at[:, lanes(owner(move) * wide, wide)], out)
                for move, out in zip(moves, outs)
            ],
            sems,
        )
        for copy in copies:
            copy.wait()

    return pl.pallas_call(
        body,
        name="pack",
        out_shape=[jax.ShapeDtypeStruct((rows, wide), value.dtype)] * count,
        in_specs=[ANY] * (1 + len(after)),
        out_specs=[VMEM] * count,
        scratch_shapes=[pltpu.SemaphoreType.DMA((count,))],
        compiler_params=pltpu.CompilerParams(vmem_limit_bytes=4 * 2**20),
        cost_estimate=pl.CostEstimate(
            flops=0, bytes_accessed=4 * count * rows * wide, transcendentals=0
        ),
    )(value, *after)


def stack(pieces, skip, take, after=()):
    rows = pieces[0].shape[0]
    count = len(pieces)

    def body(*refs):
        sources = refs[:count]
        out, held, in_sems, out_sem = refs[count + len(after) :]
        arriving = whole(
            [
                (source.at[:, pl.ds(skip, take)], held.at[pl.ds(i * rows, rows)])
                for i, source in enumerate(sources)
            ],
            in_sems,
        )
        for copy in arriving:
            copy.wait()
        leaving = pltpu.make_async_copy(held, out, out_sem)
        leaving.start()
        leaving.wait()

    return pl.pallas_call(
        body,
        name="stack",
        out_shape=jax.ShapeDtypeStruct((count * rows, take), pieces[0].dtype),
        in_specs=[ANY] * (count + len(after)),
        out_specs=ANY,
        scratch_shapes=[
            pltpu.VMEM((count * rows, take), pieces[0].dtype),
            pltpu.SemaphoreType.DMA((count,)),
            pltpu.SemaphoreType.DMA,
        ],
        compiler_params=pltpu.CompilerParams(vmem_limit_bytes=4 * 2**20),
        cost_estimate=pl.CostEstimate(
            flops=0, bytes_accessed=4 * count * rows * take, transcendentals=0
        ),
    )(*pieces, *after)


def hold(values, after):
    count = len(values)

    def body(*refs):
        del refs

    return pl.pallas_call(
        body,
        name="hold",
        out_shape=[jax.ShapeDtypeStruct(value.shape, value.dtype) for value in values],
        in_specs=[ANY] * (count + len(after)),
        out_specs=[ANY] * count,
        input_output_aliases={i: i for i in range(count)},
        compiler_params=pltpu.CompilerParams(vmem_limit_bytes=2**20),
    )(*values, *after)


def mixes(plan_ref, refresh_ref, blocks):
    chosen = refresh_ref[lax.axis_index("window")]
    plan = [plan_ref[b].astype(jnp.float32) for b in range(blocks)]
    before = [jnp.where(b < chosen, plan[b], 0.0) for b in range(blocks)]
    after = [jnp.where(b > chosen, plan[b], 0.0) for b in range(blocks)]
    return before, after


def prepare(latents, cached, plan, refresh, gain, wide, after):
    blocks = cached.shape[0]
    frames, spots, width = latents.shape
    count = len(MOVES)
    step = 3
    rows = step * spots

    def body(plan_ref, refresh_ref, latents_ref, cached_ref, gain_ref, *refs):
        outs, values_ref = refs[len(after) : -1], refs[-1]
        before, _ = mixes(plan_ref, refresh_ref, blocks)
        for i in range(step):
            hidden = latents_ref[i].astype(jnp.float32)
            for b in range(blocks):
                hidden = hidden + before[b] * cached_ref[b, i].astype(jnp.float32)
            mean_square = jnp.mean(hidden * hidden, axis=-1, keepdims=True)
            values = hidden * lax.rsqrt(mean_square + 1e-06) * gain_ref[...]
            values_ref[pl.ds(i * spots, spots), :] = values.astype(values_ref.dtype)
        for move, out in zip(MOVES, outs):
            out[...] = values_ref[:, lanes(owner(move) * wide, wide)]

    return pl.pallas_call(
        body,
        name="prepare",
        grid=(frames // step,),
        out_shape=[jax.ShapeDtypeStruct((frames * spots, wide), jnp.bfloat16)] * count,
        in_specs=[
            SMEM,
            SMEM,
            pl.BlockSpec((step, spots, width), lambda f: (f, 0, 0)),
            pl.BlockSpec((blocks, step, spots, width), lambda f: (0, f, 0, 0)),
            pl.BlockSpec((1, width), lambda f: (0, 0)),
        ]
        + [ANY] * len(after),
        out_specs=[pl.BlockSpec((rows, wide), lambda f: (f, 0))] * count,
        scratch_shapes=[pltpu.VMEM((rows, width), jnp.bfloat16)],
        compiler_params=pltpu.CompilerParams(vmem_limit_bytes=16 * 2**20),
        cost_estimate=pl.CostEstimate(
            flops=20 * latents.size, bytes_accessed=12 * latents.size, transcendentals=0
        ),
    )(plan, refresh, latents, cached, gain, *after)


def add(latents, cached, plan, refresh, wide, parts):
    blocks = cached.shape[0]
    frames, spots, width = latents.shape
    count = len(MOVES)
    step = 3
    rows = step * spots

    def body(plan_ref, refresh_ref, latents_ref, cached_ref, *refs):
        laters, later_ref = refs[:-1], refs[-1]
        before, after = mixes(plan_ref, refresh_ref, blocks)
        for i in range(step):
            later = latents_ref[i].astype(jnp.float32)
            for b in range(blocks):
                later = later + (before[b] + after[b]) * cached_ref[b, i].astype(jnp.float32)
            later_ref[pl.ds(i * spots, spots), :] = later
        for i, move in enumerate(MOVES):
            start = owner(move) * wide
            for take, later in zip(parts, laters):
                later[:, pl.ds(i * take, take)] = later_ref[:, lanes(start, take)]
                start += take

    return pl.pallas_call(
        body,
        name="add",
        grid=(frames // step,),
        out_shape=[
            jax.ShapeDtypeStruct((frames * spots, count * take), jnp.float32) for take in parts
        ],
        in_specs=[
            SMEM,
            SMEM,
            pl.BlockSpec((step, spots, width), lambda f: (f, 0, 0)),
            pl.BlockSpec((blocks, step, spots, width), lambda f: (0, f, 0, 0)),
        ],
        out_specs=[pl.BlockSpec((rows, count * take), lambda f: (f, 0)) for take in parts],
        scratch_shapes=[pltpu.VMEM((rows, width), jnp.float32)],
        compiler_params=pltpu.CompilerParams(vmem_limit_bytes=24 * 2**20),
        cost_estimate=pl.CostEstimate(
            flops=10 * latents.size, bytes_accessed=14 * latents.size, transcendentals=0
        ),
    )(plan, refresh, latents, cached)


def attend(asked, keys, values, skip, take):
    rows = asked[0].shape[0]
    count, places = len(asked), len(keys)
    pieces = [(piece, 0, skip) for piece in asked] + keys + values
    arrays = list({id(piece[0]): piece[0] for piece in pieces}.values())
    index = {id(array): i for i, array in enumerate(arrays)}
    where = [(index[id(array)], row, col) for array, row, col in pieces]
    scale = math.log2(math.e) / math.sqrt(HEAD_DIM)
    unroll = 2

    def body(*refs):
        sources, outs = refs[: len(arrays)], refs[len(arrays) :]

        def rows_of(chosen, first):
            return jnp.concatenate(
                [
                    sources[i][pl.ds(row, rows), lanes(col + first, HEAD_DIM)]
                    for i, row, col in chosen
                ],
                axis=0,
            )

        @pl.loop(0, take // (unroll * HEAD_DIM))
        def _(step):
            for u in range(unroll):
                first = (step * unroll + u) * HEAD_DIM
                query = rows_of(where[:count], first)
                key = rows_of(where[count : count + places], first)
                value = rows_of(where[count + places :], first)
                scores = lax.dot_general(
                    query, key, (((1,), (1,)), ((), ())), preferred_element_type=jnp.float32
                )
                peak = jnp.max(scores, axis=1, keepdims=True)
                weights = jnp.exp2((scores - peak) * scale).astype(jnp.bfloat16)
                both = jnp.concatenate([value, jnp.ones_like(value)], axis=1)
                total = jnp.dot(weights, both, preferred_element_type=jnp.float32)
                result = (total[:, :HEAD_DIM] / total[:, HEAD_DIM:]).astype(jnp.bfloat16)
                for i, out in enumerate(outs):
                    out[:, lanes(first, HEAD_DIM)] = result[i * rows : (i + 1) * rows]

    work = count * rows * places * rows * take
    return pl.pallas_call(
        body,
        name="attend",
        out_shape=[jax.ShapeDtypeStruct((rows, take), jnp.bfloat16)] * count,
        in_specs=[VMEM] * len(arrays),
        out_specs=[VMEM] * count,
        compiler_params=pltpu.CompilerParams(vmem_limit_bytes=24 * 2**20),
        cost_estimate=pl.CostEstimate(
            flops=8 * work,
            bytes_accessed=12 * places * rows * take,
            transcendentals=work // HEAD_DIM,
        ),
    )(*arrays)


def join(later, gate, attended, frames, wide, skip):
    count = len(MOVES)
    rows, take = attended[0].shape
    spots = rows // frames
    ends = MAXOV * spots
    sizes = (ends, rows - 2 * ends, ends)

    def body(later_ref, gate_ref, *refs):
        pieces, outs = refs[:count], refs[count:]
        for i, move in enumerate(MOVES):
            span = pl.ds(i * take, take)
            gates = gate_ref[:, lanes(owner(move) * wide + skip, take)]
            pre = later_ref[:, span] + gates * pieces[i][...].astype(jnp.float32)
            pre, start = pre.astype(jnp.bfloat16), 0
            for out, size in zip(outs, sizes):
                out[:, span] = pre[start : start + size]
                start += size

    return pl.pallas_call(
        body,
        name="join",
        out_shape=[jax.ShapeDtypeStruct((size, count * take), jnp.bfloat16) for size in sizes],
        in_specs=[VMEM] * (2 + count),
        out_specs=[VMEM] * 3,
        compiler_params=pltpu.CompilerParams(vmem_limit_bytes=8 * 2**20),
        cost_estimate=pl.CostEstimate(
            flops=2 * later.size, bytes_accessed=8 * later.size, transcendentals=0
        ),
    )(later, gate, *attended)


def blend(intersections, first, middle, last, from_prev, from_next, frames, wide, skip, before):
    count = len(MOVES)
    take = first.shape[1] // count
    ends = first.shape[0]
    spots = ends // MAXOV
    rows = frames * spots

    def body(overlaps_ref, *refs):
        first_ref, middle_ref, last_ref, prev, after = refs[:5]
        out_ref, result, out_sems = refs[-3:]
        window, windows = lax.axis_index("window"), lax.axis_size("window")
        ov_next = overlaps_ref[window]
        ov_prev = overlaps_ref[lax.rem(window + windows - 1, windows)]
        result[pl.ds(ends, rows - 2 * ends), :] = middle_ref[...]
        for f in range(MAXOV):
            ramp = jnp.where(
                f < ov_prev, jnp.float32(f + 1) / (ov_prev + 1).astype(jnp.float32), 1.0
            )
            other = jnp.clip(MAXOV - ov_prev + f, 0, MAXOV - 1) * spots
            mixed = (1.0 - ramp) * prev[pl.ds(pl.multiple_of(other, 16), spots), :].astype(
                jnp.float32
            ) + ramp * first_ref[pl.ds(f * spots, spots), :].astype(jnp.float32)
            result[pl.ds(f * spots, spots), :] = mixed.astype(result.dtype)
        for f in range(frames - MAXOV, frames):
            tail = f - frames + ov_next
            ramp = jnp.where(
                tail >= 0,
                (tail + 1).astype(jnp.float32) / (ov_next + 1).astype(jnp.float32),
                0.0,
            )
            other = jnp.clip(tail, 0, MAXOV - 1) * spots
            own = pl.ds((f - frames + MAXOV) * spots, spots)
            mixed = (1.0 - ramp) * last_ref[own, :].astype(jnp.float32) + ramp * after[
                pl.ds(pl.multiple_of(other, 16), spots), :
            ].astype(jnp.float32)
            result[pl.ds(f * spots, spots), :] = mixed.astype(result.dtype)
        leaving = whole(
            [
                (
                    result.at[:, pl.ds(i * take, take)],
                    out_ref.at[:, lanes(owner(move) * wide + skip, take)],
                )
                for i, move in enumerate(MOVES)
            ],
            out_sems,
        )
        for copy in leaving:
            copy.wait()

    extra = () if before is None else (before,)
    return pl.pallas_call(
        body,
        name="blend",
        out_shape=jax.ShapeDtypeStruct((rows, count * wide), jnp.bfloat16),
        in_specs=[SMEM] + [VMEM] * 5 + [ANY] * len(extra),
        out_specs=ANY,
        input_output_aliases={6: 0} if extra else {},
        scratch_shapes=[
            pltpu.VMEM((rows, count * take), jnp.bfloat16),
            pltpu.SemaphoreType.DMA((count,)),
        ],
        compiler_params=pltpu.CompilerParams(vmem_limit_bytes=6 * 2**20),
        cost_estimate=pl.CostEstimate(
            flops=4 * rows * count * take,
            bytes_accessed=8 * rows * count * take,
            transcendentals=0,
        ),
    )(intersections, first, middle, last, from_prev, from_next, *extra)


def shift(value, steps):
    count = lax.axis_size("window")
    pairs = [(source, (source + steps) % count) for source in range(count)]
    return lax.ppermute(value, "window", pairs)


def spread(pieces, how):
    return [how(piece, move) if move else piece for piece, move in zip(pieces, MOVES)]


def on_device(
    latents, queries, attn_keys, cached, plan, refresh, value_gain, attn_gate, intersections
):
    _, frames, spots, width = latents.shape
    rows = frames * spots
    wide = width // len(MOVES)
    parts = [heads * HEAD_DIM for heads in PARTS]
    skips = [sum(parts[:i]) for i in range(len(parts))]
    queries = queries.reshape(rows, width)
    gate = attn_gate.reshape(1, width)
    latents, cached = latents[0], cached[:, 0]
    attn_keys = attn_keys.reshape(rows, width)
    packed = [*pack(attn_keys, wide, MOVES[:1])]
    packed += pack(attn_keys, wide, MOVES[1:], packed)
    value, *values = prepare(
        latents, cached, plan, refresh, value_gain.reshape(1, width), wide, packed[:1]
    )
    far_keys = [across(packed[0])]
    keys = spread(packed, send)
    far_value = across(value)
    keys[1:3] = hold(keys[1:3], (value,))
    far_keys += [across(key) for key in keys[1:3]]
    values[:2] = hold(values[:2], (keys[1], far_keys[0]))
    values[2:] = hold(values[2:], (far_value,))
    values = spread([value, *values], send)
    asked = spread(pack(queries, wide, MOVES, (*values[1:3], *far_keys[1:2])), send)
    laters = add(latents, cached, plan, refresh, wide, parts)
    moved = [keys[3], *values[1:]]
    sends = [
        (
            across(stack(moved[:1], skips[0], parts[0], (far_keys[1], far_value, *laters))),
            across(stack(moved[1:], skips[0], parts[0], far_keys[2:])),
        ),
        *((across(stack(moved, skip, take, asked[1:2])),) for skip, take in zip(skips[1:], parts[1:])),
    ]
    rests = [
        [(rest, row, 0) for rest in sent for row in range(0, rest.shape[0], rows)] for sent in sends
    ]
    out = None
    for later, rest, skip, take in zip(laters, rests, skips, parts):
        key_places = [(key, 0, skip) for key in keys + far_keys] + rest[:1]
        value_places = [(value, 0, skip) for value in [*values, far_value]] + rest[1:]
        attended = spread(attend(asked, key_places, value_places, skip, take), send_back)
        first, middle, last = join(later, gate, attended, frames, wide, skip)
        from_prev = shift(last, 1)
        from_next = shift(first, -1)
        out = blend(
            intersections, first, middle, last, from_prev, from_next, frames, wide, skip, out
        )
    return out.reshape(1, frames, spots, width)


def solution(mesh):
    in_specs = (
        P("window", None, "token", None),
        P("window", None, "token", None),
        P("window", None, "token", None),
        P(None, "window", None, "token", None),
        P(),
        P(),
        P(),
        P(),
        P(),
    )
    out_specs = P("window", None, "token", None)
    return jax.shard_map(
        on_device, mesh=mesh, in_specs=in_specs, out_specs=out_specs, check_vma=False
    )
```

```python
import math

import jax
import jax.numpy as jnp
from jax import lax
from jax.experimental import pallas as pl
from jax.experimental.pallas import tpu as pltpu
from jax.sharding import PartitionSpec as P

HEAD_DIM = 128
MAXOV = 4
XS, YS = 2, 4
MOVES = (0, 1, 3, 2)
ANY = pl.BlockSpec(memory_space=pl.ANY)
SMEM = pl.BlockSpec(memory_space=pltpu.SMEM)
VMEM = pl.BlockSpec(memory_space=pltpu.VMEM)
VMEM_BYTES = 56 * 2**20
PARTS = (6, 4)


def send(value, move):
    pairs = [(x * YS + y, x * YS + (y + move) % YS) for x in range(XS) for y in range(YS)]
    return lax.ppermute(value, "token", pairs)


def send_back(value, move):
    return send(value, YS - move)


def across(value):
    half = XS // 2
    pairs = [(x * YS + y, (x + half) % XS * YS + y) for x in range(XS) for y in range(YS)]
    return lax.ppermute(value, "token", pairs)


def owner(move):
    return lax.rem(lax.axis_index("token") + move, YS)


def lanes(start, size):
    return pl.ds(pl.multiple_of(start, HEAD_DIM), size)


def whole(refs, sems):
    copies = [pltpu.make_async_copy(a, b, sems.at[i]) for i, (a, b) in enumerate(refs)]
    for copy in copies:
        copy.start()
    return copies


def pack(value, wide, moves, after=()):
    rows = value.shape[0]
    count = len(moves)

    def body(value_ref, *refs):
        outs, sems = refs[len(after) : -1], refs[-1]
        copies = whole(
            [
                (value_ref.at[:, lanes(owner(move) * wide, wide)], out)
                for move, out in zip(moves, outs)
            ],
            sems,
        )
        for copy in copies:
            copy.wait()

    return pl.pallas_call(
        body,
        name="pack",
        out_shape=[jax.ShapeDtypeStruct((rows, wide), value.dtype)] * count,
        in_specs=[ANY] * (1 + len(after)),
        out_specs=[VMEM] * count,
        scratch_shapes=[pltpu.SemaphoreType.DMA((count,))],
        compiler_params=pltpu.CompilerParams(vmem_limit_bytes=4 * 2**20),
        cost_estimate=pl.CostEstimate(
            flops=0, bytes_accessed=4 * count * rows * wide, transcendentals=0
        ),
    )(value, *after)


def stack(pieces, skip, take, after=()):
    rows = pieces[0].shape[0]
    count = len(pieces)

    def body(*refs):
        sources = refs[:count]
        out, held, in_sems, out_sem = refs[count + len(after) :]
        arriving = whole(
            [
                (source.at[:, pl.ds(skip, take)], held.at[pl.ds(i * rows, rows)])
                for i, source in enumerate(sources)
            ],
            in_sems,
        )
        for copy in arriving:
            copy.wait()
        leaving = pltpu.make_async_copy(held, out, out_sem)
        leaving.start()
        leaving.wait()

    return pl.pallas_call(
        body,
        name="stack",
        out_shape=jax.ShapeDtypeStruct((count * rows, take), pieces[0].dtype),
        in_specs=[ANY] * (count + len(after)),
        out_specs=ANY,
        scratch_shapes=[
            pltpu.VMEM((count * rows, take), pieces[0].dtype),
            pltpu.SemaphoreType.DMA((count,)),
            pltpu.SemaphoreType.DMA,
        ],
        compiler_params=pltpu.CompilerParams(vmem_limit_bytes=4 * 2**20),
        cost_estimate=pl.CostEstimate(
            flops=0, bytes_accessed=4 * count * rows * take, transcendentals=0
        ),
    )(*pieces, *after)


def hold(values, after):
    count = len(values)

    def body(*refs):
        del refs

    return pl.pallas_call(
        body,
        name="hold",
        out_shape=[jax.ShapeDtypeStruct(value.shape, value.dtype) for value in values],
        in_specs=[ANY] * (count + len(after)),
        out_specs=[ANY] * count,
        input_output_aliases={i: i for i in range(count)},
        compiler_params=pltpu.CompilerParams(vmem_limit_bytes=2**20),
    )(*values, *after)


def mixes(plan_ref, refresh_ref, blocks):
    chosen = refresh_ref[lax.axis_index("window")]
    plan = [plan_ref[b].astype(jnp.float32) for b in range(blocks)]
    before = [jnp.where(b < chosen, plan[b], 0.0) for b in range(blocks)]
    after = [jnp.where(b > chosen, plan[b], 0.0) for b in range(blocks)]
    return before, after


def prepare(latents, cached, plan, refresh, gain, wide, after):
    blocks = cached.shape[0]
    frames, spots, width = latents.shape
    count = len(MOVES)
    step = 3
    rows = step * spots

    def body(plan_ref, refresh_ref, latents_ref, cached_ref, gain_ref, *refs):
        outs, values_ref = refs[len(after) : -1], refs[-1]
        before, _ = mixes(plan_ref, refresh_ref, blocks)
        for i in range(step):
            hidden = latents_ref[i].astype(jnp.float32)
            for b in range(blocks):
                hidden = hidden + before[b] * cached_ref[b, i].astype(jnp.float32)
            mean_square = jnp.mean(hidden * hidden, axis=-1, keepdims=True)
            values = hidden * lax.rsqrt(mean_square + 1e-06) * gain_ref[...]
            values_ref[pl.ds(i * spots, spots), :] = values.astype(values_ref.dtype)
        for move, out in zip(MOVES, outs):
            out[...] = values_ref[:, lanes(owner(move) * wide, wide)]

    return pl.pallas_call(
        body,
        name="prepare",
        grid=(frames // step,),
        out_shape=[jax.ShapeDtypeStruct((frames * spots, wide), jnp.bfloat16)] * count,
        in_specs=[
            SMEM,
            SMEM,
            pl.BlockSpec((step, spots, width), lambda f: (f, 0, 0)),
            pl.BlockSpec((blocks, step, spots, width), lambda f: (0, f, 0, 0)),
            pl.BlockSpec((1, width), lambda f: (0, 0)),
        ]
        + [ANY] * len(after),
        out_specs=[pl.BlockSpec((rows, wide), lambda f: (f, 0))] * count,
        scratch_shapes=[pltpu.VMEM((rows, width), jnp.bfloat16)],
        compiler_params=pltpu.CompilerParams(vmem_limit_bytes=16 * 2**20),
        cost_estimate=pl.CostEstimate(
            flops=20 * latents.size, bytes_accessed=12 * latents.size, transcendentals=0
        ),
    )(plan, refresh, latents, cached, gain, *after)


def add(latents, cached, plan, refresh, wide, parts):
    blocks = cached.shape[0]
    frames, spots, width = latents.shape
    count = len(MOVES)
    step = 3
    rows = step * spots

    def body(plan_ref, refresh_ref, latents_ref, cached_ref, *refs):
        laters, later_ref = refs[:-1], refs[-1]
        before, after = mixes(plan_ref, refresh_ref, blocks)
        for i in range(step):
            later = latents_ref[i].astype(jnp.float32)
            for b in range(blocks):
                later = later + (before[b] + after[b]) * cached_ref[b, i].astype(jnp.float32)
            later_ref[pl.ds(i * spots, spots), :] = later
        for i, move in enumerate(MOVES):
            start = owner(move) * wide
            for take, later in zip(parts, laters):
                later[:, pl.ds(i * take, take)] = later_ref[:, lanes(start, take)]
                start += take

    return pl.pallas_call(
        body,
        name="add",
        grid=(frames // step,),
        out_shape=[
            jax.ShapeDtypeStruct((frames * spots, count * take), jnp.float32) for take in parts
        ],
        in_specs=[
            SMEM,
            SMEM,
            pl.BlockSpec((step, spots, width), lambda f: (f, 0, 0)),
            pl.BlockSpec((blocks, step, spots, width), lambda f: (0, f, 0, 0)),
        ],
        out_specs=[pl.BlockSpec((rows, count * take), lambda f: (f, 0)) for take in parts],
        scratch_shapes=[pltpu.VMEM((rows, width), jnp.float32)],
        compiler_params=pltpu.CompilerParams(vmem_limit_bytes=24 * 2**20),
        cost_estimate=pl.CostEstimate(
            flops=10 * latents.size, bytes_accessed=14 * latents.size, transcendentals=0
        ),
    )(plan, refresh, latents, cached)


def attend(asked, keys, values, skip, take):
    rows = asked[0].shape[0]
    count, places = len(asked), len(keys)
    pieces = [(piece, 0, skip) for piece in asked] + keys + values
    arrays = list({id(piece[0]): piece[0] for piece in pieces}.values())
    index = {id(array): i for i, array in enumerate(arrays)}
    where = [(index[id(array)], row, col) for array, row, col in pieces]
    scale = math.log2(math.e) / math.sqrt(HEAD_DIM)
    unroll = 2

    def body(*refs):
        sources, outs = refs[: len(arrays)], refs[len(arrays) :]

        def rows_of(chosen, first):
            return jnp.concatenate(
                [
                    sources[i][pl.ds(row, rows), lanes(col + first, HEAD_DIM)]
                    for i, row, col in chosen
                ],
                axis=0,
            )

        @pl.loop(0, take // (unroll * HEAD_DIM))
        def _(step):
            for u in range(unroll):
                first = (step * unroll + u) * HEAD_DIM
                query = rows_of(where[:count], first)
                key = rows_of(where[count : count + places], first)
                value = rows_of(where[count + places :], first)
                scores = lax.dot_general(
                    query, key, (((1,), (1,)), ((), ())), preferred_element_type=jnp.float32
                )
                peak = jnp.max(scores, axis=1, keepdims=True)
                weights = jnp.exp2((scores - peak) * scale).astype(jnp.bfloat16)
                both = jnp.concatenate([value, jnp.ones_like(value)], axis=1)
                total = jnp.dot(weights, both, preferred_element_type=jnp.float32)
                result = (total[:, :HEAD_DIM] / total[:, HEAD_DIM:]).astype(jnp.bfloat16)
                for i, out in enumerate(outs):
                    out[:, lanes(first, HEAD_DIM)] = result[i * rows : (i + 1) * rows]

    work = count * rows * places * rows * take
    return pl.pallas_call(
        body,
        name="attend",
        out_shape=[jax.ShapeDtypeStruct((rows, take), jnp.bfloat16)] * count,
        in_specs=[VMEM] * len(arrays),
        out_specs=[VMEM] * count,
        compiler_params=pltpu.CompilerParams(vmem_limit_bytes=24 * 2**20),
        cost_estimate=pl.CostEstimate(
            flops=8 * work,
            bytes_accessed=12 * places * rows * take,
            transcendentals=work // HEAD_DIM,
        ),
    )(*arrays)


def join(later, gate, attended, frames, wide, skip):
    count = len(MOVES)
    rows, take = attended[0].shape
    spots = rows // frames
    ends = MAXOV * spots
    sizes = (ends, rows - 2 * ends, ends)

    def body(later_ref, gate_ref, *refs):
        pieces, outs = refs[:count], refs[count:]
        for i, move in enumerate(MOVES):
            span = pl.ds(i * take, take)
            gates = gate_ref[:, lanes(owner(move) * wide + skip, take)]
            pre = later_ref[:, span] + gates * pieces[i][...].astype(jnp.float32)
            pre, start = pre.astype(jnp.bfloat16), 0
            for out, size in zip(outs, sizes):
                out[:, span] = pre[start : start + size]
                start += size

    return pl.pallas_call(
        body,
        name="join",
        out_shape=[jax.ShapeDtypeStruct((size, count * take), jnp.bfloat16) for size in sizes],
        in_specs=[VMEM] * (2 + count),
        out_specs=[VMEM] * 3,
        compiler_params=pltpu.CompilerParams(vmem_limit_bytes=8 * 2**20),
        cost_estimate=pl.CostEstimate(
            flops=2 * later.size, bytes_accessed=8 * later.size, transcendentals=0
        ),
    )(later, gate, *attended)


def blend(intersections, first, middle, last, from_prev, from_next, frames, wide, skip, before):
    count = len(MOVES)
    take = first.shape[1] // count
    ends = first.shape[0]
    spots = ends // MAXOV
    rows = frames * spots

    def body(overlaps_ref, *refs):
        first_ref, middle_ref, last_ref, prev, after = refs[:5]
        out_ref, result, out_sems = refs[-3:]
        window, windows = lax.axis_index("window"), lax.axis_size("window")
        ov_next = overlaps_ref[window]
        ov_prev = overlaps_ref[lax.rem(window + windows - 1, windows)]
        result[pl.ds(ends, rows - 2 * ends), :] = middle_ref[...]
        for f in range(MAXOV):
            ramp = jnp.where(
                f < ov_prev, jnp.float32(f + 1) / (ov_prev + 1).astype(jnp.float32), 1.0
            )
            other = jnp.clip(MAXOV - ov_prev + f, 0, MAXOV - 1) * spots
            mixed = (1.0 - ramp) * prev[pl.ds(pl.multiple_of(other, 16), spots), :].astype(
                jnp.float32
            ) + ramp * first_ref[pl.ds(f * spots, spots), :].astype(jnp.float32)
            result[pl.ds(f * spots, spots), :] = mixed.astype(result.dtype)
        for f in range(frames - MAXOV, frames):
            tail = f - frames + ov_next
            ramp = jnp.where(
                tail >= 0,
                (tail + 1).astype(jnp.float32) / (ov_next + 1).astype(jnp.float32),
                0.0,
            )
            other = jnp.clip(tail, 0, MAXOV - 1) * spots
            own = pl.ds((f - frames + MAXOV) * spots, spots)
            mixed = (1.0 - ramp) * last_ref[own, :].astype(jnp.float32) + ramp * after[
                pl.ds(pl.multiple_of(other, 16), spots), :
            ].astype(jnp.float32)
            result[pl.ds(f * spots, spots), :] = mixed.astype(result.dtype)
        leaving = whole(
            [
                (
                    result.at[:, pl.ds(i * take, take)],
                    out_ref.at[:, lanes(owner(move) * wide + skip, take)],
                )
                for i, move in enumerate(MOVES)
            ],
            out_sems,
        )
        for copy in leaving:
            copy.wait()

    extra = () if before is None else (before,)
    return pl.pallas_call(
        body,
        name="blend",
        out_shape=jax.ShapeDtypeStruct((rows, count * wide), jnp.bfloat16),
        in_specs=[SMEM] + [VMEM] * 5 + [ANY] * len(extra),
        out_specs=ANY,
        input_output_aliases={6: 0} if extra else {},
        scratch_shapes=[
            pltpu.VMEM((rows, count * take), jnp.bfloat16),
            pltpu.SemaphoreType.DMA((count,)),
        ],
        compiler_params=pltpu.CompilerParams(vmem_limit_bytes=6 * 2**20),
        cost_estimate=pl.CostEstimate(
            flops=4 * rows * count * take,
            bytes_accessed=8 * rows * count * take,
            transcendentals=0,
        ),
    )(intersections, first, middle, last, from_prev, from_next, *extra)


def shift(value, steps):
    count = lax.axis_size("window")
    pairs = [(source, (source + steps) % count) for source in range(count)]
    return lax.ppermute(value, "window", pairs)


def spread(pieces, how):
    return [how(piece, move) if move else piece for piece, move in zip(pieces, MOVES)]


def on_device(
    latents, queries, attn_keys, cached, plan, refresh, value_gain, attn_gate, intersections
):
    _, frames, spots, width = latents.shape
    rows = frames * spots
    wide = width // len(MOVES)
    parts = [heads * HEAD_DIM for heads in PARTS]
    skips = [sum(parts[:i]) for i in range(len(parts))]
    queries = queries.reshape(rows, width)
    gate = attn_gate.reshape(1, width)
    latents, cached = latents[0], cached[:, 0]
    attn_keys = attn_keys.reshape(rows, width)
    packed = [*pack(attn_keys, wide, MOVES[:1])]
    packed += pack(attn_keys, wide, MOVES[1:], packed)
    value, *values = prepare(
        latents, cached, plan, refresh, value_gain.reshape(1, width), wide, packed[:1]
    )
    far_keys = [across(packed[0])]
    keys = spread(packed, send)
    far_value = across(value)
    keys[1:3] = hold(keys[1:3], (value,))
    far_keys += [across(key) for key in keys[1:3]]
    values[:2] = hold(values[:2], (keys[1], far_keys[0]))
    values[2:] = hold(values[2:], (far_value,))
    values = spread([value, *values], send)
    asked = spread(pack(queries, wide, MOVES, (*values[1:3], *far_keys[1:2])), send)
    laters = add(latents, cached, plan, refresh, wide, parts)
    moved = [keys[3], *values[1:]]
    sends = [
        (
            across(stack(moved[:1], skips[0], parts[0], (far_keys[1], far_value))),
            across(stack(moved[1:], skips[0], parts[0], (*far_keys[2:], *laters))),
        ),
        *((across(stack(moved, skip, take, asked[1:2])),) for skip, take in zip(skips[1:], parts[1:])),
    ]
    rests = [
        [(rest, row, 0) for rest in sent for row in range(0, rest.shape[0], rows)] for sent in sends
    ]
    out = None
    for later, rest, skip, take in zip(laters, rests, skips, parts):
        key_places = [(key, 0, skip) for key in keys + far_keys] + rest[:1]
        value_places = [(value, 0, skip) for value in [*values, far_value]] + rest[1:]
        attended = spread(attend(asked, key_places, value_places, skip, take), send_back)
        first, middle, last = join(later, gate, attended, frames, wide, skip)
        from_prev = shift(last, 1)
        from_next = shift(first, -1)
        out = blend(
            intersections, first, middle, last, from_prev, from_next, frames, wide, skip, out
        )
    return out.reshape(1, frames, spots, width)


def solution(mesh):
    in_specs = (
        P("window", None, "token", None),
        P("window", None, "token", None),
        P("window", None, "token", None),
        P(None, "window", None, "token", None),
        P(),
        P(),
        P(),
        P(),
        P(),
    )
    out_specs = P("window", None, "token", None)
    return jax.shard_map(
        on_device, mesh=mesh, in_specs=in_specs, out_specs=out_specs, check_vma=False
    )
```
